128 devices in a mesh: row: 16 (over y_hi, z, core), col: 8 (over y_lo, x).
Axes of the slice: x: 4, y: 4 (y_hi: 2, y_lo: 2; y = y_hi * 2 + y_lo), z: 4, core: 2. Of those that a mesh axis runs over, the one named last changes fastest.
Arguments:
- features: bfloat16 [65536, 128], P(('row', 'col')), may hold values from -12 to 12
- tile_values: bfloat16 [16, 8, 512, 128, 128], P('row', 'col'), as said below
- tile_rows: int32 [16, 8, 512], P('row', 'col'), may hold values from 0 to 63, as said below
- tile_cols: int32 [16, 8, 512], P('row', 'col'), may hold values from 0 to 31
- tile_count: int32 [16, 8], P('row', 'col'), may hold values from 64 to 512, as said below
- weight1: bfloat16 [128, 256], replicated, may hold values from -0.5 to 0.5
- bias1: float32 [256], replicated, may hold values from -1 to 1
- weight2: bfloat16 [256, 256], replicated
- bias2: float32 [256], replicated, may hold values from -3 to 3
Outputs:
- node_out: bfloat16 [65536, 256], P(('row', 'col'))
The draws below stay inside these ranges and needn't reach their ends.
Inputs may be any that keep to these rules, and one draw needn't show every extreme that they name: The pairs (tile_rows, tile_cols) of one device are distinct. Slots 0 to tile_count - 1 of a device hold its nonempty tiles; later slots are padding. `tile_values`: entries are nonnegative.
All inputs are finite; a program needn't handle non-finite values.
Results may differ from the reference program's by a relative error of at most 0.0037.
Values may be sent and summed in bfloat16 or wider, within the bound.
No kernel may reach another device: no remote copies, remote signals or barrier semaphores. Data moves between devices by JAX's collectives and lax.ppermute only.
A program may use at most 192 MiB of HBM per device.

```python
import jax
import jax.numpy as jnp
from jax import lax

B = 128
F = 128
H = 256
NODE_DEV = 512
TMAX = 512
NODES = 65536
N_ROW = 16
N_COL = 8


def tile_layout(key):
    row_blocks = NODE_DEV * N_ROW // B
    col_blocks = NODE_DEV * N_COL // B
    positions = row_blocks * col_blocks
    device_keys = jax.random.split(key, N_ROW * N_COL)
    chosen = jax.vmap(lambda single: jax.random.permutation(single, positions)[:TMAX])(device_keys)
    return (chosen.reshape(N_ROW, N_COL, TMAX).astype(jnp.int32), col_blocks)


def draw_tile_rows(key, part):
    chosen, col_blocks = tile_layout(key)
    return (chosen // col_blocks).astype(jnp.int32)


def draw_tile_cols(key, part):
    chosen, col_blocks = tile_layout(key)
    return (chosen % col_blocks).astype(jnp.int32)


def draw_tile_count(key, part):
    key = jax.random.fold_in(key, 7)
    counts = jax.random.randint(key, (N_ROW * N_COL,), TMAX // 8, TMAX // 2 + 1).astype(jnp.int32)
    busiest = jax.random.randint(jax.random.fold_in(key, 1), (4,), 0, N_ROW * N_COL)
    counts = counts.at[busiest].set(TMAX)
    return counts.reshape(N_ROW, N_COL).astype(jnp.int32)


def draw_tile_values(key, part):
    key = jax.random.fold_in(key, 11)
    shape = (N_ROW, N_COL, TMAX, B, B)
    row_place = lax.broadcasted_iota(jnp.float32, shape, 0)
    col_place = lax.broadcasted_iota(jnp.float32, shape, 1)
    rising = (1.0 + 2.0 * row_place / max(N_ROW - 1, 1)) * (1.0 + 2.0 * col_place / max(N_COL - 1, 1))
    density = min(1.0, 12.0 * NODE_DEV / (0.3125 * TMAX * B * B))
    uniform_draw = jax.random.uniform(key, shape, jnp.float32)
    scaled = uniform_draw / density
    entry = (0.25 + 0.75 * scaled) * rising
    return jnp.where(uniform_draw < density, entry, 0.0).astype(jnp.bfloat16)


def draw_weight2(key, part):
    key = jax.random.fold_in(key, 13)
    shape = (H, H)
    first_place = lax.broadcasted_iota(jnp.int32, shape, 0)
    second_place = lax.broadcasted_iota(jnp.int32, shape, 1)
    on_diagonal = (first_place == second_place).astype(jnp.float32)
    diagonal_scale = jnp.exp(jax.random.uniform(jax.random.fold_in(key, 1), shape, jnp.float32, -0.35, 0.35))
    spread = jax.random.normal(key, shape, jnp.float32)
    entry = on_diagonal * diagonal_scale + 0.4 * spread / H ** 0.5
    return entry.astype(jnp.bfloat16)


def block_levels(own_key, extent, cuts, low, top_value):
    def one(dim, blocks):
        draws = jax.random.uniform(jax.random.fold_in(jax.random.fold_in(own_key, 6), dim), (blocks,), jnp.float32, low / len(cuts), top_value / len(cuts))
        return jnp.repeat(jnp.exp(draws), extent[dim] // blocks).reshape((-1,) + (1,) * (len(extent) - dim - 1))

    level = one(*cuts[0])
    for cut in cuts[1:]:
        level = level * one(*cut)
    return level


def noise(own_key, shape, width, limit, cuts=(), held_as=jnp.bfloat16):
    level = block_levels(own_key, shape, cuts, -0.22, 0.18) if cuts else 1.0
    result = jax.random.normal(own_key, shape, jnp.float32) * width * level
    return jnp.minimum(jnp.maximum(result, -limit), limit).astype(held_as)


def setup_inputs(seed: int = 0) -> dict:
    key_list = jax.random.split(jax.random.key(seed), 10)
    return {
        "features": noise(key_list[0], (NODES, F), 2.0, 12.0, ((0, 128),)),
        "tile_values": draw_tile_values(jax.random.fold_in(key_list[9], 71), 0),
        "tile_rows": draw_tile_rows(jax.random.fold_in(key_list[9], 71), 0),
        "tile_cols": draw_tile_cols(jax.random.fold_in(key_list[9], 71), 0),
        "tile_count": draw_tile_count(jax.random.fold_in(key_list[9], 71), 0),
        "weight1": noise(key_list[5], (F, H), F ** -0.5, 0.5),
        "bias1": noise(key_list[6], (H,), 0.2, 1.0, (), jnp.float32),
        "weight2": draw_weight2(jax.random.fold_in(key_list[9], 71), 0),
        "bias2": noise(key_list[8], (H,), 0.5, 3.0, (), jnp.float32),
    }


def reference(features, tile_values, tile_rows, tile_cols, tile_count, weight1, bias1, weight2, bias2):
    node_total = features.shape[0]
    row_blocks = NODE_DEV * N_ROW // B
    col_blocks = NODE_DEV * N_COL // B
    device_total = N_ROW * N_COL

    def aggregate(source, transposed):
        source_width = source.shape[1]
        source_blocks = source.reshape(-1, B, source_width).astype(jnp.float32)

        def advance(state, device):
            summed, degree = state
            row_index = device // N_COL
            col_index = device % N_COL
            tile_block = tile_values[row_index, col_index].astype(jnp.float32)
            out_rows = col_index * row_blocks + tile_rows[row_index, col_index]
            in_cols = row_index * col_blocks + tile_cols[row_index, col_index]
            live_mask = (jnp.arange(TMAX, dtype=jnp.int32) < tile_count[row_index, col_index]).astype(jnp.float32)
            if transposed:
                picked = source_blocks[out_rows]
                products = jnp.einsum("kab,kaw->kbw", tile_block, picked)
                tile_sums = jnp.sum(tile_block, axis=1)
                target = in_cols
            else:
                picked = source_blocks[in_cols]
                products = jnp.einsum("kab,kbw->kaw", tile_block, picked)
                tile_sums = jnp.sum(tile_block, axis=2)
                target = out_rows
            summed = summed.at[target].add(products * live_mask[:, None, None])
            degree = degree.at[target].add(tile_sums * live_mask[:, None])
            return (summed, degree), None

        initial = (jnp.zeros((node_total // B, B, source_width), jnp.float32),
                   jnp.zeros((node_total // B, B), jnp.float32))
        (summed, degree), _ = lax.scan(advance, initial, jnp.arange(device_total, dtype=jnp.int32))
        summed = summed.reshape(node_total, source_width) + source.astype(jnp.float32)
        return summed / (1.0 + degree.reshape(node_total))[:, None]

    first_mean = aggregate(features, False).astype(jnp.bfloat16)
    hidden = jax.nn.relu(jnp.dot(first_mean, weight1, preferred_element_type=jnp.float32) + bias1).astype(jnp.bfloat16)
    second_mean = aggregate(hidden, True).astype(jnp.bfloat16)
    return (jnp.dot(second_mean, weight2, preferred_element_type=jnp.float32) + bias2).astype(jnp.bfloat16)
```

```python
import functools

import jax
import jax.numpy as jnp
from jax import lax
from jax.experimental import pallas as pl
from jax.experimental.pallas import tpu as pltpu
from jax.sharding import PartitionSpec as P

F32 = jnp.float32
BF16 = jnp.bfloat16
I32 = jnp.int32
TILE = 128
EXTRA = 16
UNROLL = 8
CHUNK = 32


def dot(a, b, dims):
    return lax.dot_general(a, b, (dims, ((), ())), preferred_element_type=F32)


def order_by(key_row, key_col, other_col, slot_col, live_col, blocks, length, other_span):
    slots = key_col.shape[0]
    lane_block = lax.broadcasted_iota(I32, (slots, 128), 1)
    hot = jnp.where((key_col == lane_block) & (live_col > 0), 1.0, 0.0)
    before = jnp.where(
        lax.broadcasted_iota(I32, (slots, slots), 1) < lax.broadcasted_iota(I32, (slots, slots), 0), 1.0, 0.0
    )
    prefix = dot(before.astype(BF16), hot.astype(BF16), ((1,), (0,)))
    rank = jnp.sum(hot * prefix, axis=1, keepdims=True)
    count = jnp.sum(hot, axis=0, keepdims=True)
    pairs = jnp.floor((count + 1.0) * 0.5)
    below = jnp.where(
        lax.broadcasted_iota(I32, (128, 128), 0) < lax.broadcasted_iota(I32, (128, 128), 1), 1.0, 0.0
    )
    start = dot(jnp.broadcast_to(pairs, (8, 128)).astype(BF16), below.astype(BF16), ((1,), (0,)))[0:1]
    place = 2.0 * jnp.sum(hot * start, axis=1, keepdims=True) + rank
    place = jnp.where(live_col > 0, place, -1.0).astype(I32)
    empty = slots * other_span
    code = slot_col * other_span + other_col - empty
    where_to = lax.broadcasted_iota(I32, (slots, length), 1)
    codes = jnp.sum(jnp.where(place == where_to, code, 0), axis=0, keepdims=True) + empty
    start_col = jnp.transpose(jnp.broadcast_to(start, (8, 128)))[:, 0:1]
    block_id = lax.broadcasted_iota(I32, (128, length), 0)
    pair_id = lax.broadcasted_iota(I32, (128, length), 1).astype(F32)
    reached = (start_col <= pair_id) & (block_id < blocks)
    out_block = jnp.sum(jnp.where(reached, 1, 0), axis=0, keepdims=True) - 1
    total = jnp.sum(pairs, axis=1, keepdims=True).astype(I32)
    return codes, out_block, total


def order_kernel(row_blocks, col_blocks, count_ref, index_ref, list_ref):
    slots = index_ref.shape[1]
    length = list_ref.shape[1]
    turned = jnp.transpose(index_ref[...].astype(F32)).astype(I32)
    row_col, col_col = turned[:, 0:1], turned[:, 1:2]
    slot_col = lax.broadcasted_iota(I32, (slots, 1), 0)
    live_col = jnp.where(slot_col < count_ref[0, 0], 1, 0)
    lists = []
    for key, other, blocks, span in (
        (row_col, col_col, row_blocks, 64),
        (col_col, row_col, col_blocks, 64),
    ):
        codes, out_block, total = order_by(None, key, other, slot_col, live_col, blocks, length, span)
        lists += [codes, out_block, jnp.broadcast_to(total, (1, length))]
    list_ref[...] = jnp.concatenate(lists + [lists[0], lists[0]], axis=0)


def load_tiles(values_ref, tiles, sems, count):
    slots = values_ref.shape[0]
    steps = slots // CHUNK
    copies = [
        pltpu.make_async_copy(
            values_ref.at[pl.ds(i * CHUNK, CHUNK)], tiles.at[pl.ds(i * CHUNK, CHUNK)], sems.at[i]
        )
        for i in range(steps)
    ]
    for i, copy in enumerate(copies):
        pl.when(i * CHUNK < count)(copy.start)
    tiles[slots] = jnp.zeros(tiles.shape[1:], tiles.dtype)

    def finish():
        for i, copy in enumerate(copies):
            pl.when(i * CHUNK < count)(copy.wait)

    return finish


def run_pairs(list_ref, first, tiles, source, acc, tile_dims):
    total = list_ref[first + 2, 0]
    ones = jnp.ones((EXTRA, 2 * TILE), BF16)

    def step(i, carry):
        sums = []
        for u in range(UNROLL):
            q = i * UNROLL + u
            code0 = list_ref[first, 2 * q]
            code1 = list_ref[first, 2 * q + 1]
            left = jnp.concatenate([source[code0 & 63], source[code1 & 63]], axis=1)
            left = jnp.concatenate([left, ones], axis=0)
            axis = 0 if tile_dims == 0 else 1
            right = jnp.concatenate([tiles[code0 >> 6], tiles[code1 >> 6]], axis=axis)
            sums.append(dot(left, right, ((1,), (tile_dims,))))
        for u in range(UNROLL):
            block = list_ref[first + 1, i * UNROLL + u]
            acc[block] += sums[u]
        return carry

    lax.fori_loop(0, (total + UNROLL - 1) // UNROLL, step, 0)


def write_partials(acc, out_ref, per_dest, width):
    def one(d, carry):
        tails = []
        for j in range(per_dest):
            block = acc[d * per_dest + j]
            out_ref[d, pl.ds(j * width, width), :] = block[:width].astype(BF16)
            degree = block[width : width + 1]
            high = degree.astype(BF16).astype(F32)
            tails += [high, degree - high]
        tails.append(jnp.zeros((EXTRA - 2 * per_dest, TILE), F32))
        out_ref[d, pl.ds(per_dest * width, EXTRA), :] = jnp.concatenate(tails, axis=0).astype(BF16)
        return carry

    lax.fori_loop(0, out_ref.shape[0], one, 0)


def own_region(per_row):
    row, col = lax.axis_index("row"), lax.axis_index("col")
    return row // per_row == col, row % per_row


def first_kernel(per_row, count_ref, list_ref, source_ref, values_ref, out_ref, tiles, acc, sems):
    finish = load_tiles(values_ref, tiles, sems, count_ref[0, 0])
    acc[...] = jnp.zeros_like(acc)
    own, part = own_region(per_row)
    col_blocks = source_ref.shape[0]

    @pl.when(own)
    def _():
        def add(j, carry):
            acc[part * col_blocks + j, pl.ds(0, TILE), :] = source_ref[j].astype(F32)
            return carry

        lax.fori_loop(0, col_blocks, add, 0)

    finish()
    run_pairs(list_ref, 0, tiles, source_ref, acc, 1)
    write_partials(acc, out_ref, acc.shape[0] // out_ref.shape[0], TILE)


def second_kernel(
    per_row, count_ref, list_ref, mean_ref, weight_ref, bias_ref, values_ref, out_ref, tiles, acc, hidden, sems
):
    finish = load_tiles(values_ref, tiles, sems, count_ref[0, 0])
    width = hidden.shape[1]
    bias = jnp.broadcast_to(bias_ref[...], (width, TILE))

    def transform(j, carry):
        for u in range(4):
            part = dot(weight_ref[...], mean_ref[j * 4 + u], ((1,), (0,)))
            hidden[j * 4 + u] = jnp.maximum(part + bias, 0.0).astype(BF16)
        return carry

    lax.fori_loop(0, hidden.shape[0] // 4, transform, 0)
    acc[...] = jnp.zeros_like(acc)
    own, part = own_region(per_row)
    col_blocks = acc.shape[0]

    @pl.when(own)
    def _():
        def add(j, carry):
            acc[j, pl.ds(0, width), :] = hidden[part * col_blocks + j].astype(F32)
            return carry

        lax.fori_loop(0, col_blocks, add, 0)

    finish()
    run_pairs(list_ref, 3, tiles, hidden, acc, 0)
    write_partials(acc, out_ref, acc.shape[0] // out_ref.shape[0], width)


def total_mean(parts_ref, j, per_dest, width):
    sources = parts_ref.shape[0]
    block = parts_ref[0, pl.ds(j * width, width), :].astype(F32)
    for s in range(1, sources):
        block += parts_ref[s, pl.ds(j * width, width), :].astype(F32)
    tail = parts_ref[0, pl.ds(per_dest * width, EXTRA), :].astype(F32)
    for s in range(1, sources):
        tail += parts_ref[s, pl.ds(per_dest * width, EXTRA), :].astype(F32)
    degree = 1.0 + (tail[2 * j : 2 * j + 1] + tail[2 * j + 1 : 2 * j + 2])
    return (block / degree).astype(BF16)


def mean_kernel(per_dest, parts_ref, out_ref):
    for j in range(per_dest):
        mean = total_mean(parts_ref, j, per_dest, TILE)
        for d in range(out_ref.shape[0]):
            out_ref[d, j] = mean


def last_kernel(per_dest, width, parts_ref, weight_ref, bias_ref, out_ref):
    for j in range(per_dest):
        mean = total_mean(parts_ref, j, per_dest, width)
        result = dot(mean, weight_ref[...], ((0,), (0,))) + bias_ref[...]
        out_ref[pl.ds(j * TILE, TILE), :] = result.astype(BF16)


def call(kernel, out, specs, scratch=(), limit=16):
    return pl.pallas_call(
        kernel,
        out_shape=out,
        in_specs=specs,
        out_specs=pl.BlockSpec(memory_space=pltpu.VMEM),
        scratch_shapes=scratch,
        compiler_params=pltpu.CompilerParams(vmem_limit_bytes=limit * 1024 * 1024),
    )


def local(features, tile_values, tile_rows, tile_cols, tile_count, weight1, bias1, weight2, bias2):
    n_row, n_col = lax.axis_size("row"), lax.axis_size("col")
    rows_dev, in_width = features.shape
    width = weight1.shape[1]
    values = tile_values[0, 0]
    slots = values.shape[0]
    per_dev = rows_dev // TILE
    row_blocks, col_blocks = per_dev * n_row, per_dev * n_col
    per_row = n_row // n_col
    count = tile_count.astype(I32)
    vmem = pl.BlockSpec(memory_space=pltpu.VMEM)
    smem = pl.BlockSpec(memory_space=pltpu.SMEM)
    anywhere = pl.BlockSpec(memory_space=pl.ANY)

    index = jnp.concatenate([tile_rows[0], tile_cols[0], jnp.zeros((6, slots), I32)], axis=0)
    length = -(-(slots + row_blocks + 2 * UNROLL) // 128) * 128
    lists = call(
        functools.partial(order_kernel, row_blocks, col_blocks),
        jax.ShapeDtypeStruct((8, length), I32),
        [smem, vmem],
    )(count, index)

    turned = jnp.swapaxes(features.reshape(per_dev, TILE, in_width), 1, 2)
    gathered = lax.all_to_all(jnp.broadcast_to(turned[None], (n_col,) + turned.shape), "col", 0, 0)
    source = gathered.reshape(col_blocks, in_width, TILE)

    tiles = pltpu.VMEM((slots + 1, TILE, TILE), BF16)
    sems = pltpu.SemaphoreType.DMA((slots // CHUNK,))
    first = call(
        functools.partial(first_kernel, per_row),
        jax.ShapeDtypeStruct((n_row, per_dev * in_width + EXTRA, TILE), BF16),
        [smem, smem, vmem, anywhere],
        [tiles, pltpu.VMEM((row_blocks, in_width + EXTRA, TILE), F32), sems],
        48,
    )(count, lists, source, values)
    first = lax.all_to_all(first, "row", 0, 0)
    mean = call(
        functools.partial(mean_kernel, per_dev),
        jax.ShapeDtypeStruct((n_row, per_dev, in_width, TILE), BF16),
        [vmem],
    )(first)
    means = lax.all_to_all(mean, "row", 0, 0).reshape(row_blocks, in_width, TILE)
    second = call(
        functools.partial(second_kernel, per_row),
        jax.ShapeDtypeStruct((n_col, per_dev * width + EXTRA, TILE), BF16),
        [smem, smem, vmem, vmem, vmem, anywhere],
        [
            tiles,
            pltpu.VMEM((col_blocks, width + EXTRA, TILE), F32),
            pltpu.VMEM((row_blocks, width, TILE), BF16),
            sems,
        ],
        48,
    )(count, lists, means, weight1.T, bias1.reshape(width, 1), values)
    second = lax.all_to_all(second, "col", 0, 0)
    return call(
        functools.partial(last_kernel, per_dev, width),
        jax.ShapeDtypeStruct((rows_dev, width), BF16),
        [vmem, vmem, vmem],
    )(second, weight2, bias2.reshape(1, width))


def solution(mesh):
    in_specs = (
        P(("row", "col"), None),
        P("row", "col", None, None, None),
        P("row", "col", None),
        P("row", "col", None),
        P("row", "col"),
        P(),
        P(),
        P(),
        P(),
    )
    out_specs = P(("row", "col"), None)
    return jax.shard_map(local, mesh=mesh, in_specs=in_specs, out_specs=out_specs, check_vma=False)
```

```python
import functools

import jax
import jax.numpy as jnp
from jax import lax
from jax.experimental import pallas as pl
from jax.experimental.pallas import tpu as pltpu
from jax.sharding import PartitionSpec as P

F32 = jnp.float32
BF16 = jnp.bfloat16
I32 = jnp.int32
TILE = 128
EXTRA = 16
UNROLL = 16
CHUNK = 32
SPAN = 64
CORES = 2
FAR_FIRST = (6, 5, 7, 2, 4, 1, 3)


def dot(a, b, dims):
    return lax.dot_general(a, b, (dims, ((), ())), preferred_element_type=F32)


def order_by(key, source, slot, live, keys, length):
    slots = key.shape[0]
    half = keys // 2
    lane = lax.broadcasted_iota(I32, (slots, 128), 1)
    hot = jnp.where((key == lane) & live, 1.0, 0.0)
    earlier = lax.broadcasted_iota(I32, (slots, slots), 1) < lax.broadcasted_iota(I32, (slots, slots), 0)
    prefix = dot(jnp.where(earlier, 1.0, 0.0).astype(BF16), hot.astype(BF16), ((1,), (0,)))
    rank = jnp.sum(hot * prefix, axis=1, keepdims=True)
    count = jnp.sum(hot, axis=0, keepdims=True)
    pairs = jnp.floor((count + 1.0) * 0.5)
    from_key = lax.broadcasted_iota(I32, (128, 128), 0)
    to_key = lax.broadcasted_iota(I32, (128, 128), 1)
    below = jnp.where((from_key < to_key) & ((from_key >= half) | (to_key < half)), 1.0, 0.0)
    start = dot(jnp.broadcast_to(pairs, (8, 128)).astype(BF16), below.astype(BF16), ((1,), (0,)))[0:1]
    first_half = lax.broadcasted_iota(I32, (1, 128), 1) < half
    pairs0 = jnp.sum(jnp.where(first_half, pairs, 0.0), axis=1, keepdims=True)
    pairs1 = jnp.sum(jnp.where(first_half, 0.0, pairs), axis=1, keepdims=True)
    steps0 = jnp.floor((pairs0 + (UNROLL - 1.0)) * (1.0 / UNROLL))
    steps1 = steps0 + jnp.floor((pairs1 + (UNROLL - 1.0)) * (1.0 / UNROLL))
    start = start + jnp.where(first_half, 0.0, steps0 * UNROLL)
    place = 2.0 * jnp.sum(hot * start, axis=1, keepdims=True) + rank
    place = jnp.where(live, place, -1.0).astype(I32)
    empty = slots * SPAN
    code = slot * SPAN + source - empty
    position = lax.broadcasted_iota(I32, (slots, length), 1)
    codes = jnp.sum(jnp.where(place == position, code, 0), axis=0, keepdims=True) + empty
    start_col = jnp.transpose(jnp.broadcast_to(start, (8, 128)))[:, 0:1]
    key_id = lax.broadcasted_iota(I32, (128, length), 0)
    pair_id = lax.broadcasted_iota(I32, (128, length), 1).astype(F32)
    reached = (start_col <= pair_id) & (key_id < keys)
    out_key = jnp.sum(jnp.where(reached, 1, 0), axis=0, keepdims=True) - 1
    out_block = jnp.where(out_key >= half, out_key - half, out_key)
    return codes, out_block, steps0.astype(I32), steps1.astype(I32)


def turn_kernel(features_ref, out_ref):
    for j in range(out_ref.shape[0]):
        out_ref[j] = jnp.transpose(features_ref[pl.ds(j * TILE, TILE), :])


def order_kernel(
    per_dev,
    row_blocks,
    col_blocks,
    count_ref,
    rows_ref,
    cols_ref,
    weight_ref,
    bias_ref,
    values_ref,
    list_ref,
    tiles,
    weight_out,
    bias_out,
    sems,
):
    slots = rows_ref.shape[1]
    length = list_ref.shape[1]
    count = count_ref[0, 0]
    copies = [
        pltpu.make_async_copy(
            values_ref.at[pl.ds(i * CHUNK, CHUNK)], tiles.at[pl.ds(i * CHUNK, CHUNK)], sems.at[i]
        )
        for i in range(slots // CHUNK)
    ]
    for i, copy in enumerate(copies):
        pl.when(i * CHUNK < count)(copy.start)
    tiles[slots] = jnp.zeros(tiles.shape[1:], tiles.dtype)

    weight_out[...] = jnp.transpose(weight_ref[...])
    bias_out[...] = jnp.transpose(jnp.broadcast_to(bias_ref[...], (TILE, bias_ref.shape[1])))
    index = jnp.concatenate([rows_ref[...], cols_ref[...], jnp.zeros((6, slots), I32)], axis=0)
    turned = jnp.transpose(index.astype(F32)).astype(I32)
    row, col = turned[:, 0:1], turned[:, 1:2]
    slot = lax.broadcasted_iota(I32, (slots, 1), 0)
    live = slot < count
    core = lax.axis_index("row") % CORES
    owner = row // per_dev
    in_half = (owner // CORES) * per_dev + row % per_dev
    own = (owner % CORES) == core
    half_rows = row_blocks // CORES
    lane = lax.broadcasted_iota(I32, (1, length), 1)
    rows = []
    for key, source, keys in (
        (jnp.where(own, half_rows, 0) + in_half, col, row_blocks),
        (jnp.where(own, 0, col_blocks) + col, in_half, 2 * col_blocks),
    ):
        codes, out_block, steps0, steps1 = order_by(key, source, slot, live, keys, length)
        rows += [codes, out_block, jnp.where(lane == 0, steps0, steps1)]
    list_ref[...] = jnp.concatenate(rows + [jnp.zeros((2, length), I32)], axis=0)
    for i, copy in enumerate(copies):
        pl.when(i * CHUNK < count)(copy.wait)


def run_pairs(list_ref, first, half, tiles, source, acc, tile_dims):
    ones = jnp.ones((EXTRA, 2 * TILE), BF16)

    def step(i, carry):
        sums = []
        for u in range(UNROLL):
            q = i * UNROLL + u
            code0 = list_ref[first, 2 * q]
            code1 = list_ref[first, 2 * q + 1]
            left = jnp.concatenate([source[code0 & (SPAN - 1)], source[code1 & (SPAN - 1)]], axis=1)
            left = jnp.concatenate([left, ones], axis=0)
            right = jnp.concatenate([tiles[code0 // SPAN], tiles[code1 // SPAN]], axis=tile_dims)
            sums.append(dot(left, right, ((1,), (tile_dims,))))
        for u in range(UNROLL):
            acc[list_ref[first + 1, i * UNROLL + u]] += sums[u]
        return carry

    begin = 0 if half == 0 else list_ref[first + 2, 0]
    lax.fori_loop(begin, list_ref[first + 2, half], step, 0)


def parted(degree):
    high = degree.astype(BF16).astype(F32)
    return [high, degree - high]


def write_partials(block_of, out, d, per_dest, width):
    tails = []
    for j in range(per_dest):
        block, degree = block_of(d, j)
        out[pl.ds(j * width, width), :] = block.astype(BF16)
        tails += parted(degree)
    tails.append(jnp.zeros((EXTRA - 2 * per_dest, TILE), F32))
    out[pl.ds(per_dest * width, EXTRA), :] = jnp.concatenate(tails, axis=0).astype(BF16)


def on_diagonal(per_dev, other, add):
    row, col = lax.axis_index("row"), lax.axis_index("col")
    core = row % CORES
    which = 1 - core if other else core

    @pl.when(row // CORES == col)
    def _():
        def one(i, carry):
            m, t = i // per_dev, i % per_dev
            in_half = (core * per_dev + m) * per_dev + t
            add(in_half, (m * CORES + which) * per_dev + t)
            return carry

        lax.fori_loop(0, per_dev * per_dev, one, 0)


def lay_out(me, per_dev, pieces, out):
    for m, piece in enumerate(pieces):
        out[pl.ds((me ^ m) * per_dev, per_dev)] = piece[...]


def first_kernel(per_dev, half, n_col, list_ref, *refs):
    if half == 0:
        pieces, (tiles, out_ref, source, acc) = refs[:n_col], refs[n_col:]
        lay_out(lax.axis_index("col"), per_dev, pieces, source)
    else:
        source, tiles, acc = refs
    acc[...] = jnp.zeros_like(acc)

    def add(in_half, col_block):
        acc[in_half, pl.ds(0, TILE), :] = source[col_block].astype(F32)

    on_diagonal(per_dev, half == 0, add)
    run_pairs(list_ref, 0, half, tiles, source, acc, 1)
    if half == 0:

        def block_of(d, j):
            block = acc[d * per_dev + j]
            return block[:TILE], block[TILE : TILE + 1]

        def one(d, carry):
            write_partials(block_of, out_ref.at[d], d, per_dev, TILE)
            return carry

        lax.fori_loop(0, out_ref.shape[0], one, 0)


def join_kernel(per_dev, acc, parts_ref, *outs):
    def block_of(d, j):
        block = acc[d * per_dev + j]
        tail = parts_ref[d, pl.ds(per_dev * TILE, EXTRA), :].astype(F32)
        degree = block[TILE : TILE + 1] + (tail[2 * j : 2 * j + 1] + tail[2 * j + 1 : 2 * j + 2])
        return block[:TILE] + parts_ref[d, pl.ds(j * TILE, TILE), :].astype(F32), degree

    chip = lax.axis_index("row") // CORES
    for m, out in enumerate(outs):
        write_partials(block_of, out, chip ^ m, per_dev, TILE)


def gather_kernel(per_dev, *refs):
    lay_out(lax.axis_index("row") // CORES, per_dev, refs[:-1], refs[-1])


def second_kernel(per_dev, half, list_ref, mean_ref, weight_ref, bias_ref, tiles, *refs):
    if half == 0:
        out_ref, hidden = refs
        acc = out_ref
    else:
        before, out_ref, hidden, acc = refs
    width = hidden.shape[1]
    bias = jnp.concatenate([bias_ref[...], bias_ref[...]], axis=1)

    def transform(i, carry):
        for u in range(2):
            b = 4 * i + 2 * u
            means = jnp.concatenate([mean_ref[b], mean_ref[b + 1]], axis=1)
            both = jnp.maximum(dot(weight_ref[...], means, ((1,), (0,))) + bias, 0.0).astype(BF16)
            hidden[b] = both[:, :TILE]
            hidden[b + 1] = both[:, TILE:]
        return carry

    lax.fori_loop(0, hidden.shape[0] // 4, transform, 0)
    acc[...] = jnp.zeros_like(acc)

    def add(in_half, col_block):
        acc[col_block, pl.ds(0, width), :] = hidden[in_half].astype(F32)

    on_diagonal(per_dev, half == 1, add)
    run_pairs(list_ref, 3, half, tiles, hidden, acc, 0)
    if half == 1:

        def block_of(d, j):
            block = acc[d * per_dev + j] + before[d * per_dev + j]
            return block[:width], block[width : width + 1]

        def one(d, carry):
            write_partials(block_of, out_ref.at[d], d, per_dev, width)
            return carry

        lax.fori_loop(0, out_ref.shape[0], one, 0)


def total_mean(parts, j, per_dest, width):
    block = parts[0][pl.ds(j * width, width), :].astype(F32)
    tail = parts[0][pl.ds(per_dest * width, EXTRA), :].astype(F32)
    for part in parts[1:]:
        block += part[pl.ds(j * width, width), :].astype(F32)
        tail += part[pl.ds(per_dest * width, EXTRA), :].astype(F32)
    degree = 1.0 + (tail[2 * j : 2 * j + 1] + tail[2 * j + 1 : 2 * j + 2])
    return (block / degree).astype(BF16)


def mean_kernel(per_dest, *refs):
    parts, out_ref = refs[:-1], refs[-1]
    for j in range(per_dest):
        out_ref[j] = total_mean(parts, j, per_dest, TILE)


def last_kernel(per_dest, width, weight_ref, bias_ref, parts_ref, out_ref):
    parts = [parts_ref.at[s] for s in range(parts_ref.shape[0])]
    for j in range(per_dest):
        mean = total_mean(parts, j, per_dest, width)
        result = dot(mean, weight_ref[...], ((0,), (0,))) + bias_ref[...]
        out_ref[pl.ds(j * TILE, TILE), :] = result.astype(BF16)


def call(kernel, out, specs, scratch=(), limit=8, us=1):
    vmem = pl.BlockSpec(memory_space=pltpu.VMEM)
    return pl.pallas_call(
        kernel,
        out_shape=out,
        in_specs=specs,
        out_specs=jax.tree.map(lambda _: vmem, out),
        scratch_shapes=scratch,
        cost_estimate=pl.CostEstimate(flops=us * 10**9, bytes_accessed=us * 3 * 10**6, transcendentals=0),
        compiler_params=pltpu.CompilerParams(vmem_limit_bytes=limit * 1024 * 1024),
    )


def local(features, tile_values, tile_rows, tile_cols, tile_count, weight1, bias1, weight2, bias2):
    n_row, n_col = lax.axis_size("row"), lax.axis_size("col")
    rows_dev, in_width = features.shape
    width = weight1.shape[1]
    values = tile_values[0, 0]
    slots = values.shape[0]
    per_dev = rows_dev // TILE
    row_blocks, col_blocks = per_dev * n_row, per_dev * n_col
    half_rows = row_blocks // CORES
    chips = n_row // CORES
    count = tile_count.astype(I32)
    vmem = pl.BlockSpec(memory_space=pltpu.VMEM)
    smem = pl.BlockSpec(memory_space=pltpu.SMEM)
    hbm = pl.BlockSpec(memory_space=pltpu.HBM)
    shape = jax.ShapeDtypeStruct
    swap = [(i, i ^ 1) for i in range(n_row)]
    part = lambda rows: shape((per_dev * rows + EXTRA, TILE), BF16)

    def across(axis, n, step, pieces):
        came = {0: pieces[0]}
        for m in FAR_FIRST:
            came[m] = lax.ppermute(pieces[m], axis, [(i, i ^ (m * step)) for i in range(n)])
        return [came[m] for m in range(len(pieces))]

    turned = call(turn_kernel, shape((per_dev, in_width, TILE), BF16), [vmem])(features)
    pieces = across("col", n_col, 1, [turned] * n_col)

    length = -(-(slots + row_blocks + 4 * UNROLL) // 128) * 128
    lists, tiles, weight, bias = call(
        functools.partial(order_kernel, per_dev, row_blocks, col_blocks),
        (
            shape((8, length), I32),
            pltpu.VMEM((slots + 1, TILE, TILE), BF16),
            shape((width, in_width), BF16),
            shape((width, TILE), F32),
        ),
        [smem, vmem, vmem, vmem, vmem, hbm],
        [pltpu.SemaphoreType.DMA((slots // CHUNK,))],
        8,
        8,
    )(
        count,
        tile_rows[0],
        tile_cols[0],
        weight1,
        bias1.reshape(1, width),
        pltpu.with_memory_space_constraint(values, pltpu.HBM),
    )
    tiles = pltpu.with_memory_space_constraint(tiles, pltpu.VMEM)

    acc = (half_rows, in_width + EXTRA, TILE)
    away, source = call(
        functools.partial(first_kernel, per_dev, 0, n_col),
        (
            shape((chips, per_dev * in_width + EXTRA, TILE), BF16),
            shape((col_blocks, in_width, TILE), BF16),
        ),
        [smem] + [vmem] * (n_col + 1),
        [pltpu.VMEM(acc, F32)],
        8,
        4,
    )(lists, *pieces, tiles)
    came = lax.ppermute(away, "row", swap)
    kept = call(
        functools.partial(first_kernel, per_dev, 1, n_col), shape(acc, F32), [smem, vmem, vmem], (), 8, 4
    )(lists, source, tiles)
    first = call(
        functools.partial(join_kernel, per_dev), [part(in_width)] * chips, [vmem, vmem]
    )(kept, came)
    first = across("row", n_row, CORES, first)
    mean = call(
        functools.partial(mean_kernel, per_dev), shape((per_dev, in_width, TILE), BF16), [vmem] * chips
    )(*first)
    means = across("row", n_row, CORES, [mean] * chips)
    own = call(
        functools.partial(gather_kernel, per_dev), shape((half_rows, in_width, TILE), BF16), [vmem] * chips
    )(*means)
    other = lax.ppermute(own, "row", swap)

    acc = (col_blocks, width + EXTRA, TILE)
    hidden = pltpu.VMEM((half_rows, width, TILE), BF16)
    before = call(
        functools.partial(second_kernel, per_dev, 0),
        shape(acc, F32),
        [smem, vmem, vmem, vmem, vmem],
        [hidden],
        8,
        6,
    )(lists, own, weight, bias, tiles)
    second = call(
        functools.partial(second_kernel, per_dev, 1),
        shape((n_col, per_dev * width + EXTRA, TILE), BF16),
        [smem, vmem, vmem, vmem, vmem, vmem],
        [hidden, pltpu.VMEM(acc, F32)],
        12,
        6,
    )(lists, other, weight, bias, tiles, before)
    second = lax.all_to_all(second, "col", 0, 0)
    return call(
        functools.partial(last_kernel, per_dev, width),
        shape((rows_dev, width), BF16),
        [vmem] * 3,
    )(weight2, bias2.reshape(1, width), second)


def solution(mesh):
    in_specs = (
        P(("row", "col"), None),
        P("row", "col", None, None, None),
        P("row", "col", None),
        P("row", "col", None),
        P("row", "col"),
        P(),
        P(),
        P(),
        P(),
    )
    out_specs = P(("row", "col"), None)
    return jax.shard_map(local, mesh=mesh, in_specs=in_specs, out_specs=out_specs, check_vma=False)
```

```python
import functools

import jax
import jax.numpy as jnp
from jax import lax
from jax.experimental import pallas as pl
from jax.experimental.pallas import tpu as pltpu
from jax.sharding import PartitionSpec as P

F32 = jnp.float32
BF16 = jnp.bfloat16
I32 = jnp.int32
TILE = 128
EXTRA = 16
UNROLL = 16
CHUNK = 32
OUT = 1 << 16
SPAN = 64
CORES = 2
FAR_FIRST = (6, 5, 7, 2, 4, 1, 3)


def dot(a, b, dims):
    return lax.dot_general(a, b, (dims, ((), ())), preferred_element_type=F32)


def order_by(key, source, slot, live, earlier, keys):
    length = 3 * 128
    slots = key.shape[0]
    half = keys // 2
    lane = lax.broadcasted_iota(I32, (1, 128), 1)
    hot = jnp.where((key == lane) & live, 1.0, 0.0)
    prefix = dot(earlier, hot.astype(BF16), ((1,), (0,)))
    rank = jnp.sum(hot * prefix, axis=1, keepdims=True)
    count = jnp.sum(hot, axis=0, keepdims=True)
    pairs = jnp.floor((count + 1.0) * 0.5)
    from_key = lax.broadcasted_iota(I32, (128, 128), 0)
    to_key = lax.broadcasted_iota(I32, (128, 128), 1)
    below = jnp.where((from_key < to_key) & ((from_key >= half) | (to_key < half)), 1.0, 0.0)
    start = dot(jnp.broadcast_to(pairs, (8, 128)).astype(BF16), below.astype(BF16), ((1,), (0,)))[0:1]
    first_half = lax.broadcasted_iota(I32, (1, 128), 1) < half
    pairs0 = jnp.sum(jnp.where(first_half, pairs, 0.0), axis=1, keepdims=True)
    pairs1 = jnp.sum(jnp.where(first_half, 0.0, pairs), axis=1, keepdims=True)
    steps0 = jnp.floor((pairs0 + (UNROLL - 1.0)) * (1.0 / UNROLL))
    steps1 = steps0 + jnp.floor((pairs1 + (UNROLL - 1.0)) * (1.0 / UNROLL))
    start = start + jnp.where(first_half, 0.0, steps0 * UNROLL)
    place = 2.0 * jnp.sum(hot * start, axis=1, keepdims=True) + rank
    place = jnp.where(live, place, -1.0).astype(I32)
    empty = slots * SPAN
    code = slot * SPAN + source - empty
    position = 2 * lax.broadcasted_iota(I32, (1, length), 1)
    codes0 = jnp.sum(jnp.where(place == position, code, 0), axis=0, keepdims=True) + empty
    codes1 = jnp.sum(jnp.where(place == position + 1, code, 0), axis=0, keepdims=True) + empty
    start_col = jnp.transpose(jnp.broadcast_to(start, (8, 128)))[:, 0:1]
    key_id = lax.broadcasted_iota(I32, (128, 1), 0)
    pair_id = lax.broadcasted_iota(I32, (1, length), 1).astype(F32)
    reached = jnp.where(key_id < keys, start_col, 2.0**20) <= pair_id
    out_key = jnp.sum(jnp.where(reached, 1, 0), axis=0, keepdims=True) - 1
    out_block = jnp.where(out_key >= half, out_key - half, out_key)
    codes0 = codes0 + OUT * out_block
    rows = [codes[:, i : i + 128] for codes in (codes0, codes1) for i in range(0, length, 128)]
    rows.append(jnp.where(lane == 0, steps0, steps1).astype(I32))
    return jnp.concatenate(rows + [jnp.zeros((1, 128), I32)], axis=0)


def order_kernel(
    per_dev,
    row_blocks,
    col_blocks,
    count_ref,
    rows_ref,
    cols_ref,
    weight_ref,
    bias_ref,
    values_ref,
    first_ref,
    second_ref,
    tiles,
    weight_out,
    bias_out,
    sems,
    rows,
    cols,
    weight,
    bias,
    small_sems,
):
    slots = rows_ref.shape[1]
    count = count_ref[0, 0]
    small = [
        pltpu.make_async_copy(src, dst, small_sems.at[i])
        for i, (src, dst) in enumerate(
            ((rows_ref, rows), (cols_ref, cols), (weight_ref, weight), (bias_ref, bias))
        )
    ]
    for copy in small:
        copy.start()
    copies = [
        pltpu.make_async_copy(
            values_ref.at[pl.ds(i * CHUNK, CHUNK)], tiles.at[pl.ds(i * CHUNK, CHUNK)], sems.at[i]
        )
        for i in range(slots // CHUNK)
    ]
    for i, copy in enumerate(copies):
        pl.when(i * CHUNK < count)(functools.partial(copy.start, priority=1))
    tiles[slots] = jnp.zeros(tiles.shape[1:], tiles.dtype)

    earlier = lax.broadcasted_iota(I32, (1, slots), 1) < lax.broadcasted_iota(I32, (slots, 1), 0)
    earlier = jnp.where(earlier, 1.0, 0.0).astype(BF16)
    for copy in small:
        copy.wait()
    weight_out[...] = jnp.transpose(weight[...])
    bias_out[...] = jnp.transpose(jnp.broadcast_to(bias[...], (TILE, bias.shape[1])))
    index = jnp.concatenate([rows[...], cols[...], jnp.zeros((6, slots), I32)], axis=0)
    turned = jnp.transpose(index.astype(F32)).astype(I32)
    row, col = turned[:, 0:1], turned[:, 1:2]
    slot = lax.broadcasted_iota(I32, (slots, 1), 0)
    live = slot < count
    core = lax.axis_index("row") % CORES
    owner = row // per_dev
    in_half = (owner // CORES) * per_dev + row % per_dev
    own = (owner % CORES) == core
    half_rows = row_blocks // CORES
    key = jnp.where(own, half_rows, 0) + in_half
    first_ref[...] = order_by(key, col, slot, live, earlier, row_blocks)
    key = jnp.where(own, 0, col_blocks) + col
    second_ref[...] = order_by(key, in_half, slot, live, earlier, 2 * col_blocks)
    for i, copy in enumerate(copies):
        pl.when(i * CHUNK < count)(copy.wait)


def run_pairs(list_ref, half, tiles, source, acc, tile_dims):
    ones = jnp.ones((EXTRA, 2 * TILE), BF16)

    def step(i, carry):
        row, lane = i // (128 // UNROLL), i % (128 // UNROLL) * UNROLL
        blocks, sums = [], []
        for u in range(UNROLL):
            word = list_ref[row, lane + u]
            code0, code1 = word & (OUT - 1), list_ref[3 + row, lane + u]
            left = jnp.concatenate([source[code0 & (SPAN - 1)], source[code1 & (SPAN - 1)]], axis=1)
            left = jnp.concatenate([left, ones], axis=0)
            right = jnp.concatenate([tiles[code0 // SPAN], tiles[code1 // SPAN]], axis=tile_dims)
            blocks.append(word // OUT)
            sums.append(dot(left, right, ((1,), (tile_dims,))))
        for block, total in zip(blocks, sums):
            acc[block] += total
        return carry

    begin = 0 if half == 0 else list_ref[6, 0]
    lax.fori_loop(begin, list_ref[6, half], step, 0)


def parted(degree):
    high = degree.astype(BF16).astype(F32)
    return [high, degree - high]


def write_partials(block_of, out, d, per_dest, width):
    tails = []
    for j in range(per_dest):
        block, degree = block_of(d, j)
        out[pl.ds(j * width, width), :] = block.astype(BF16)
        tails += parted(degree)
    tails.append(jnp.zeros((EXTRA - 2 * per_dest, TILE), F32))
    out[pl.ds(per_dest * width, EXTRA), :] = jnp.concatenate(tails, axis=0).astype(BF16)


def on_diagonal(per_dev, other, add):
    row, col = lax.axis_index("row"), lax.axis_index("col")
    core = row % CORES
    which = 1 - core if other else core

    @pl.when(row // CORES == col)
    def _():
        def one(i, carry):
            m, t = i // per_dev, i % per_dev
            in_half = (core * per_dev + m) * per_dev + t
            add(in_half, (m * CORES + which) * per_dev + t)
            return carry

        lax.fori_loop(0, per_dev * per_dev, one, 0)


def lay_out(me, per_dev, pieces, out):
    for m, piece in enumerate(pieces):
        out[pl.ds((me ^ m) * per_dev, per_dev)] = piece[...]


def first_kernel(per_dev, half, n_col, list_ref, *refs):
    if half == 0:
        pieces, (tiles, out_ref, source, acc) = refs[:n_col], refs[n_col:]
        for m, piece in enumerate(pieces):
            first = (lax.axis_index("col") ^ m) * per_dev
            for j in range(per_dev):
                source[first + j] = jnp.transpose(piece[pl.ds(j * TILE, TILE), :])
    else:
        source, tiles, acc = refs
    acc[...] = jnp.zeros_like(acc)

    def add(in_half, col_block):
        acc[in_half, pl.ds(0, TILE), :] = source[col_block].astype(F32)

    on_diagonal(per_dev, half == 0, add)
    run_pairs(list_ref, half, tiles, source, acc, 1)
    if half == 0:

        def block_of(d, j):
            block = acc[d * per_dev + j]
            return block[:TILE], block[TILE : TILE + 1]

        def one(d, carry):
            write_partials(block_of, out_ref.at[d], d, per_dev, TILE)
            return carry

        lax.fori_loop(0, out_ref.shape[0], one, 0)


def join_kernel(per_dev, acc, parts_ref, *outs):
    def block_of(d, j):
        block = acc[d * per_dev + j]
        tail = parts_ref[d, pl.ds(per_dev * TILE, EXTRA), :].astype(F32)
        degree = block[TILE : TILE + 1] + (tail[2 * j : 2 * j + 1] + tail[2 * j + 1 : 2 * j + 2])
        return block[:TILE] + parts_ref[d, pl.ds(j * TILE, TILE), :].astype(F32), degree

    chip = lax.axis_index("row") // CORES
    for m, out in enumerate(outs):
        write_partials(block_of, out, chip ^ m, per_dev, TILE)


def gather_kernel(per_dev, *refs):
    lay_out(lax.axis_index("row") // CORES, per_dev, refs[:-1], refs[-1])


def second_kernel(per_dev, half, list_ref, mean_ref, weight_ref, bias_ref, tiles, *refs):
    if half == 0:
        out_ref, hidden = refs
        acc = out_ref
    else:
        before, out_ref, hidden, acc = refs
    width = hidden.shape[1]
    bias = jnp.concatenate([bias_ref[...], bias_ref[...]], axis=1)

    for b in range(0, hidden.shape[0], 2):
        means = jnp.concatenate([mean_ref[b], mean_ref[b + 1]], axis=1)
        both = jnp.maximum(dot(weight_ref[...], means, ((1,), (0,))) + bias, 0.0).astype(BF16)
        hidden[b] = both[:, :TILE]
        hidden[b + 1] = both[:, TILE:]
    acc[...] = jnp.zeros_like(acc)

    def add(in_half, col_block):
        acc[col_block, pl.ds(0, width), :] = hidden[in_half].astype(F32)

    on_diagonal(per_dev, half == 1, add)
    run_pairs(list_ref, half, tiles, hidden, acc, 0)
    if half == 1:

        def block_of(d, j):
            block = acc[d * per_dev + j] + before[d * per_dev + j]
            return block[:width], block[width : width + 1]

        def one(d, carry):
            write_partials(block_of, out_ref.at[d], d, per_dev, width)
            return carry

        lax.fori_loop(0, out_ref.shape[0], one, 0)


def total_mean(parts, j, per_dest, width):
    block = parts[0][pl.ds(j * width, width), :].astype(F32)
    tail = parts[0][pl.ds(per_dest * width, EXTRA), :].astype(F32)
    for part in parts[1:]:
        block += part[pl.ds(j * width, width), :].astype(F32)
        tail += part[pl.ds(per_dest * width, EXTRA), :].astype(F32)
    degree = 1.0 + (tail[2 * j : 2 * j + 1] + tail[2 * j + 1 : 2 * j + 2])
    return (block / degree).astype(BF16)


def mean_kernel(per_dest, *refs):
    parts, out_ref = refs[:-1], refs[-1]
    for j in range(per_dest):
        out_ref[j] = total_mean(parts, j, per_dest, TILE)


def last_kernel(per_dest, width, weight_ref, bias_ref, parts_ref, out_ref):
    parts = [parts_ref.at[s] for s in range(parts_ref.shape[0])]
    for j in range(per_dest):
        mean = total_mean(parts, j, per_dest, width)
        result = dot(mean, weight_ref[...], ((0,), (0,))) + bias_ref[...]
        out_ref[pl.ds(j * TILE, TILE), :] = result.astype(BF16)


def call(kernel, out, specs, scratch=(), limit=8, us=1):
    vmem = pl.BlockSpec(memory_space=pltpu.VMEM)
    return pl.pallas_call(
        kernel,
        out_shape=out,
        in_specs=specs,
        out_specs=jax.tree.map(lambda _: vmem, out),
        scratch_shapes=scratch,
        cost_estimate=pl.CostEstimate(flops=us * 10**9, bytes_accessed=us * 3 * 10**6, transcendentals=0),
        compiler_params=pltpu.CompilerParams(vmem_limit_bytes=limit * 1024 * 1024),
    )


def local(features, tile_values, tile_rows, tile_cols, tile_count, weight1, bias1, weight2, bias2):
    n_row, n_col = lax.axis_size("row"), lax.axis_size("col")
    rows_dev, in_width = features.shape
    width = weight1.shape[1]
    values = tile_values[0, 0]
    slots = values.shape[0]
    per_dev = rows_dev // TILE
    row_blocks, col_blocks = per_dev * n_row, per_dev * n_col
    half_rows = row_blocks // CORES
    chips = n_row // CORES
    count = tile_count.astype(I32)
    vmem = pl.BlockSpec(memory_space=pltpu.VMEM)
    smem = pl.BlockSpec(memory_space=pltpu.SMEM)
    hbm = pl.BlockSpec(memory_space=pltpu.HBM)
    shape = jax.ShapeDtypeStruct
    swap = [(i, i ^ 1) for i in range(n_row)]
    part = lambda rows: shape((per_dev * rows + EXTRA, TILE), BF16)

    def across(axis, n, step, pieces):
        came = {0: pieces[0]}
        for m in FAR_FIRST:
            came[m] = lax.ppermute(pieces[m], axis, [(i, i ^ (m * step)) for i in range(n)])
        return [came[m] for m in range(len(pieces))]

    pieces = across("col", n_col, 1, [features] * n_col)

    first_list, second_list, tiles, weight, bias = call(
        functools.partial(order_kernel, per_dev, row_blocks, col_blocks),
        (
            shape((8, 128), I32),
            shape((8, 128), I32),
            pltpu.VMEM((slots + 1, TILE, TILE), BF16),
            shape((width, in_width), BF16),
            shape((width, TILE), F32),
        ),
        [smem] + [hbm] * 5,
        [
            pltpu.SemaphoreType.DMA((slots // CHUNK,)),
            pltpu.VMEM((1, slots), I32),
            pltpu.VMEM((1, slots), I32),
            pltpu.VMEM((in_width, width), BF16),
            pltpu.VMEM((1, width), F32),
            pltpu.SemaphoreType.DMA((4,)),
        ],
        8,
        8,
    )(
        count,
        *(
            pltpu.with_memory_space_constraint(x, pltpu.HBM)
            for x in (tile_rows[0], tile_cols[0], weight1, bias1.reshape(1, width), values)
        ),
    )
    tiles = pltpu.with_memory_space_constraint(tiles, pltpu.VMEM)

    acc = (half_rows, in_width + EXTRA, TILE)
    away, source = call(
        functools.partial(first_kernel, per_dev, 0, n_col),
        (
            shape((chips, per_dev * in_width + EXTRA, TILE), BF16),
            shape((col_blocks, in_width, TILE), BF16),
        ),
        [smem] + [vmem] * (n_col + 1),
        [pltpu.VMEM(acc, F32)],
        8,
        4,
    )(first_list, *pieces, tiles)
    came = lax.ppermute(away, "row", swap)
    kept = call(
        functools.partial(first_kernel, per_dev, 1, n_col), shape(acc, F32), [smem, vmem, vmem], (), 8, 4
    )(first_list, source, tiles)
    first = call(
        functools.partial(join_kernel, per_dev), [part(in_width)] * chips, [vmem, vmem]
    )(kept, came)
    first = across("row", n_row, CORES, first)
    mean = call(
        functools.partial(mean_kernel, per_dev), shape((per_dev, in_width, TILE), BF16), [vmem] * chips
    )(*first)
    means = across("row", n_row, CORES, [mean] * chips)
    own = call(
        functools.partial(gather_kernel, per_dev), shape((half_rows, in_width, TILE), BF16), [vmem] * chips
    )(*means)
    other = lax.ppermute(own, "row", swap)

    acc = (col_blocks, width + EXTRA, TILE)
    hidden = pltpu.VMEM((half_rows, width, TILE), BF16)
    before = call(
        functools.partial(second_kernel, per_dev, 0),
        shape(acc, F32),
        [smem, vmem, vmem, vmem, vmem],
        [hidden],
        8,
        6,
    )(second_list, own, weight, bias, tiles)
    second = call(
        functools.partial(second_kernel, per_dev, 1),
        shape((n_col, per_dev * width + EXTRA, TILE), BF16),
        [smem, vmem, vmem, vmem, vmem, vmem],
        [hidden, pltpu.VMEM(acc, F32)],
        12,
        6,
    )(second_list, other, weight, bias, tiles, before)
    second = lax.all_to_all(second, "col", 0, 0)
    return call(
        functools.partial(last_kernel, per_dev, width),
        shape((rows_dev, width), BF16),
        [vmem] * 3,
    )(weight2, bias2.reshape(1, width), second)


def solution(mesh):
    in_specs = (
        P(("row", "col"), None),
        P("row", "col", None, None, None),
        P("row", "col", None),
        P("row", "col", None),
        P("row", "col"),
        P(),
        P(),
        P(),
        P(),
    )
    out_specs = P(("row", "col"), None)
    return jax.shard_map(local, mesh=mesh, in_specs=in_specs, out_specs=out_specs, check_vma=False)
```

```python
import functools

import jax
import jax.numpy as jnp
from jax import lax
from jax.experimental import pallas as pl
from jax.experimental.pallas import tpu as pltpu
from jax.sharding import PartitionSpec as P

F32 = jnp.float32
BF16 = jnp.bfloat16
I32 = jnp.int32
TILE = 128
EXTRA = 16
UNROLL = 16
CHUNK = 32
OUT = 1 << 16
SPAN = 64
CORES = 2
FAR_FIRST = (6, 5, 7, 2, 4, 1, 3)


def dot(a, b, dims):
    return lax.dot_general(a, b, (dims, ((), ())), preferred_element_type=F32)


def order_by(key, source, slot, live, earlier, keys):
    length = 3 * 128
    slots = key.shape[0]
    half = keys // 2
    lane = lax.broadcasted_iota(I32, (1, 128), 1)
    hot = jnp.where((key == lane) & live, 1.0, 0.0)
    prefix = dot(earlier, hot.astype(BF16), ((1,), (0,)))
    rank = jnp.sum(hot * prefix, axis=1, keepdims=True)
    count = jnp.sum(hot, axis=0, keepdims=True)
    pairs = jnp.floor((count + 1.0) * 0.5)
    from_key = lax.broadcasted_iota(I32, (128, 128), 0)
    to_key = lax.broadcasted_iota(I32, (128, 128), 1)
    below = jnp.where((from_key < to_key) & ((from_key >= half) | (to_key < half)), 1.0, 0.0)
    start = dot(jnp.broadcast_to(pairs, (8, 128)).astype(BF16), below.astype(BF16), ((1,), (0,)))[0:1]
    first_half = lax.broadcasted_iota(I32, (1, 128), 1) < half
    pairs0 = jnp.sum(jnp.where(first_half, pairs, 0.0), axis=1, keepdims=True)
    pairs1 = jnp.sum(jnp.where(first_half, 0.0, pairs), axis=1, keepdims=True)
    steps0 = jnp.floor((pairs0 + (UNROLL - 1.0)) * (1.0 / UNROLL))
    steps1 = steps0 + jnp.floor((pairs1 + (UNROLL - 1.0)) * (1.0 / UNROLL))
    start = start + jnp.where(first_half, 0.0, steps0 * UNROLL)
    place = 2.0 * jnp.sum(hot * start, axis=1, keepdims=True) + rank
    place = jnp.where(live, place, -1.0).astype(I32)
    empty = slots * SPAN
    code = slot * SPAN + source - empty
    position = 2 * lax.broadcasted_iota(I32, (1, length), 1)
    codes0 = jnp.sum(jnp.where(place == position, code, 0), axis=0, keepdims=True) + empty
    codes1 = jnp.sum(jnp.where(place == position + 1, code, 0), axis=0, keepdims=True) + empty
    start_col = jnp.transpose(jnp.broadcast_to(start, (8, 128)))[:, 0:1]
    key_id = lax.broadcasted_iota(I32, (128, 1), 0)
    pair_id = lax.broadcasted_iota(I32, (1, length), 1).astype(F32)
    reached = jnp.where(key_id < keys, start_col, 2.0**20) <= pair_id
    out_key = jnp.sum(jnp.where(reached, 1, 0), axis=0, keepdims=True) - 1
    out_block = jnp.where(out_key >= half, out_key - half, out_key)
    codes0 = codes0 + OUT * out_block
    rows = [codes[:, i : i + 128] for codes in (codes0, codes1) for i in range(0, length, 128)]
    rows.append(jnp.where(lane == 0, steps0, steps1).astype(I32))
    return jnp.concatenate(rows + [jnp.zeros((1, 128), I32)], axis=0)


def order_kernel(
    per_dev,
    row_blocks,
    col_blocks,
    count_ref,
    rows_ref,
    cols_ref,
    weight_ref,
    bias_ref,
    values_ref,
    first_ref,
    second_ref,
    tiles,
    weight_out,
    bias_out,
    sems,
    rows,
    cols,
    weight,
    bias,
    small_sems,
):
    slots = rows_ref.shape[1]
    count = count_ref[0, 0]
    small = [
        pltpu.make_async_copy(src, dst, small_sems.at[i])
        for i, (src, dst) in enumerate(
            ((rows_ref, rows), (cols_ref, cols), (weight_ref, weight), (bias_ref, bias))
        )
    ]
    for copy in small:
        copy.start()
    copies = [
        pltpu.make_async_copy(
            values_ref.at[pl.ds(i * CHUNK, CHUNK)], tiles.at[pl.ds(i * CHUNK, CHUNK)], sems.at[i]
        )
        for i in range(slots // CHUNK)
    ]
    for i, copy in enumerate(copies):
        pl.when(i * CHUNK < count)(functools.partial(copy.start, priority=1))
    tiles[slots] = jnp.zeros(tiles.shape[1:], tiles.dtype)

    earlier = lax.broadcasted_iota(I32, (1, slots), 1) < lax.broadcasted_iota(I32, (slots, 1), 0)
    earlier = jnp.where(earlier, 1.0, 0.0).astype(BF16)
    for copy in small:
        copy.wait()
    weight_out[...] = jnp.transpose(weight[...])
    bias_out[...] = jnp.transpose(jnp.broadcast_to(bias[...], (TILE, bias.shape[1])))
    index = jnp.concatenate([rows[...], cols[...], jnp.zeros((6, slots), I32)], axis=0)
    turned = jnp.transpose(index.astype(F32)).astype(I32)
    row, col = turned[:, 0:1], turned[:, 1:2]
    slot = lax.broadcasted_iota(I32, (slots, 1), 0)
    live = slot < count
    core = lax.axis_index("row") % CORES
    owner = row // per_dev
    in_half = (owner // CORES) * per_dev + row % per_dev
    own = (owner % CORES) == core
    half_rows = row_blocks // CORES
    key = jnp.where(own, half_rows, 0) + in_half
    first_ref[...] = order_by(key, col, slot, live, earlier, row_blocks)
    key = jnp.where(own, 0, col_blocks) + col
    second_ref[...] = order_by(key, in_half, slot, live, earlier, 2 * col_blocks)
    for i, copy in enumerate(copies):
        pl.when(i * CHUNK < count)(copy.wait)


def run_pairs(list_ref, half, tiles, source, acc, tile_dims):
    ones = jnp.ones((EXTRA, 2 * TILE), BF16)

    def step(i, carry):
        row, lane = i // (128 // UNROLL), i % (128 // UNROLL) * UNROLL
        blocks, sums = [], []
        for u in range(UNROLL):
            word = list_ref[row, lane + u]
            code0, code1 = word & (OUT - 1), list_ref[3 + row, lane + u]
            left = jnp.concatenate([source[code0 & (SPAN - 1)], source[code1 & (SPAN - 1)]], axis=1)
            left = jnp.concatenate([left, ones], axis=0)
            right = jnp.concatenate([tiles[code0 // SPAN], tiles[code1 // SPAN]], axis=tile_dims)
            blocks.append(word // OUT)
            sums.append(dot(left, right, ((1,), (tile_dims,))))
        for block, total in zip(blocks, sums):
            acc[block] += total
        return carry

    begin = 0 if half == 0 else list_ref[6, 0]
    lax.fori_loop(begin, list_ref[6, half], step, 0)


def parted(degree):
    high = degree.astype(BF16).astype(F32)
    return [high, degree - high]


def write_partials(block_of, out, d, per_dest, width):
    tails = []
    for j in range(per_dest):
        block, degree = block_of(d, j)
        out[pl.ds(j * width, width), :] = block.astype(BF16)
        tails += parted(degree)
    tails.append(jnp.zeros((EXTRA - 2 * per_dest, TILE), F32))
    out[pl.ds(per_dest * width, EXTRA), :] = jnp.concatenate(tails, axis=0).astype(BF16)


def on_diagonal(per_dev, other, add):
    row, col = lax.axis_index("row"), lax.axis_index("col")
    core = row % CORES
    which = 1 - core if other else core

    @pl.when(row // CORES == col)
    def _():
        def one(i, carry):
            m, t = i // per_dev, i % per_dev
            in_half = (core * per_dev + m) * per_dev + t
            add(in_half, (m * CORES + which) * per_dev + t)
            return carry

        lax.fori_loop(0, per_dev * per_dev, one, 0)


def lay_out(me, per_dev, pieces, out):
    for m, piece in enumerate(pieces):
        out[pl.ds((me ^ m) * per_dev, per_dev)] = piece[...]


def first_kernel(per_dev, half, n_col, list_ref, *refs):
    if half == 0:
        pieces, (tiles, out_ref, source, acc) = refs[:n_col], refs[n_col:]
        for m, piece in enumerate(pieces):
            first = (lax.axis_index("col") ^ m) * per_dev
            for j in range(per_dev):
                source[first + j] = jnp.transpose(piece[pl.ds(j * TILE, TILE), :])
    else:
        source, tiles, acc = refs
    acc[...] = jnp.zeros_like(acc)

    def add(in_half, col_block):
        acc[in_half, pl.ds(0, TILE), :] = source[col_block].astype(F32)

    on_diagonal(per_dev, half == 0, add)
    run_pairs(list_ref, half, tiles, source, acc, 1)
    if half == 0:

        def block_of(d, j):
            block = acc[d * per_dev + j]
            return block[:TILE], block[TILE : TILE + 1]

        def one(d, carry):
            write_partials(block_of, out_ref.at[d], d, per_dev, TILE)
            return carry

        lax.fori_loop(0, out_ref.shape[0], one, 0)


def join_kernel(per_dev, acc, parts_ref, *outs):
    def block_of(d, j):
        block = acc[d * per_dev + j]
        tail = parts_ref[d, pl.ds(per_dev * TILE, EXTRA), :].astype(F32)
        degree = block[TILE : TILE + 1] + (tail[2 * j : 2 * j + 1] + tail[2 * j + 1 : 2 * j + 2])
        return block[:TILE] + parts_ref[d, pl.ds(j * TILE, TILE), :].astype(F32), degree

    chip = lax.axis_index("row") // CORES
    for m, out in enumerate(outs):
        write_partials(block_of, out, chip ^ m, per_dev, TILE)


def gather_kernel(per_dev, *refs):
    lay_out(lax.axis_index("row") // CORES, per_dev, refs[:-1], refs[-1])


def second_kernel(per_dev, half, list_ref, mean_ref, weight_ref, bias_ref, tiles, *refs):
    if half == 0:
        out_ref, hidden = refs
        acc = out_ref
    else:
        before, out_ref, hidden, acc = refs
    width = hidden.shape[1]
    bias = jnp.concatenate([bias_ref[...], bias_ref[...]], axis=1)

    for b in range(0, hidden.shape[0], 2):
        means = jnp.concatenate([mean_ref[b], mean_ref[b + 1]], axis=1)
        both = jnp.maximum(dot(weight_ref[...], means, ((1,), (0,))) + bias, 0.0).astype(BF16)
        hidden[b] = both[:, :TILE]
        hidden[b + 1] = both[:, TILE:]
    acc[...] = jnp.zeros_like(acc)

    def add(in_half, col_block):
        acc[col_block, pl.ds(0, width), :] = hidden[in_half].astype(F32)

    on_diagonal(per_dev, half == 1, add)
    run_pairs(list_ref, half, tiles, hidden, acc, 0)
    if half == 1:

        def block_of(d, j):
            block = acc[d * per_dev + j] + before[d * per_dev + j]
            return block[:width], block[width : width + 1]

        def one(d, carry):
            write_partials(block_of, out_ref.at[d], d, per_dev, width)
            return carry

        lax.fori_loop(0, out_ref.shape[0], one, 0)


def total_mean(parts, j, per_dest, width):
    block = parts[0][pl.ds(j * width, width), :].astype(F32)
    tail = parts[0][pl.ds(per_dest * width, EXTRA), :].astype(F32)
    for part in parts[1:]:
        block += part[pl.ds(j * width, width), :].astype(F32)
        tail += part[pl.ds(per_dest * width, EXTRA), :].astype(F32)
    degree = 1.0 + (tail[2 * j : 2 * j + 1] + tail[2 * j + 1 : 2 * j + 2])
    return (block / degree).astype(BF16)


def mean_kernel(per_dest, *refs):
    parts, out_ref = refs[:-1], refs[-1]
    for j in range(per_dest):
        out_ref[j] = total_mean(parts, j, per_dest, TILE)


def last_kernel(per_dest, width, weight_ref, bias_ref, parts_ref, out_ref):
    parts = [parts_ref.at[s] for s in range(parts_ref.shape[0])]
    for j in range(per_dest):
        mean = total_mean(parts, j, per_dest, width)
        result = dot(mean, weight_ref[...], ((0,), (0,))) + bias_ref[...]
        out_ref[pl.ds(j * TILE, TILE), :] = result.astype(BF16)


def call(kernel, out, specs, scratch=(), limit=8, us=1):
    vmem = pl.BlockSpec(memory_space=pltpu.VMEM)
    return pl.pallas_call(
        kernel,
        out_shape=out,
        in_specs=specs,
        out_specs=jax.tree.map(lambda _: vmem, out),
        scratch_shapes=scratch,
        cost_estimate=pl.CostEstimate(flops=us * 10**9, bytes_accessed=us * 3 * 10**6, transcendentals=0),
        compiler_params=pltpu.CompilerParams(vmem_limit_bytes=limit * 1024 * 1024),
    )


def local(features, tile_values, tile_rows, tile_cols, tile_count, weight1, bias1, weight2, bias2):
    n_row, n_col = lax.axis_size("row"), lax.axis_size("col")
    rows_dev, in_width = features.shape
    width = weight1.shape[1]
    values = tile_values[0, 0]
    slots = values.shape[0]
    per_dev = rows_dev // TILE
    row_blocks, col_blocks = per_dev * n_row, per_dev * n_col
    half_rows = row_blocks // CORES
    chips = n_row // CORES
    count = tile_count.astype(I32)
    vmem = pl.BlockSpec(memory_space=pltpu.VMEM)
    smem = pl.BlockSpec(memory_space=pltpu.SMEM)
    hbm = pl.BlockSpec(memory_space=pltpu.HBM)
    shape = jax.ShapeDtypeStruct
    swap = [(i, i ^ 1) for i in range(n_row)]
    part = lambda rows: shape((per_dev * rows + EXTRA, TILE), BF16)

    def across(axis, n, step, pieces):
        came = {0: pieces[0]}
        for m in FAR_FIRST:
            came[m] = lax.ppermute(pieces[m], axis, [(i, i ^ (m * step)) for i in range(n)])
        return [came[m] for m in range(len(pieces))]

    pieces = across("col", n_col, 1, [features] * n_col)

    first_list, second_list, tiles, weight, bias = call(
        functools.partial(order_kernel, per_dev, row_blocks, col_blocks),
        (
            shape((8, 128), I32),
            shape((8, 128), I32),
            pltpu.VMEM((slots + 1, TILE, TILE), BF16),
            shape((width, in_width), BF16),
            shape((width, TILE), F32),
        ),
        [smem] + [hbm] * 5,
        [
            pltpu.SemaphoreType.DMA((slots // CHUNK,)),
            pltpu.VMEM((1, slots), I32),
            pltpu.VMEM((1, slots), I32),
            pltpu.VMEM((in_width, width), BF16),
            pltpu.VMEM((1, width), F32),
            pltpu.SemaphoreType.DMA((4,)),
        ],
        8,
        8,
    )(
        count,
        *(
            pltpu.with_memory_space_constraint(x, pltpu.HBM)
            for x in (tile_rows[0], tile_cols[0], weight1, bias1.reshape(1, width), values)
        ),
    )
    tiles = pltpu.with_memory_space_constraint(tiles, pltpu.VMEM)

    acc = (half_rows, in_width + EXTRA, TILE)
    away, source = call(
        functools.partial(first_kernel, per_dev, 0, n_col),
        (
            shape((chips, per_dev * in_width + EXTRA, TILE), BF16),
            shape((col_blocks, in_width, TILE), BF16),
        ),
        [smem] + [vmem] * (n_col + 1),
        [pltpu.VMEM(acc, F32)],
        8,
        4,
    )(first_list, *pieces, tiles)
    came = lax.ppermute(away, "row", swap)
    kept = call(
        functools.partial(first_kernel, per_dev, 1, n_col), shape(acc, F32), [smem, vmem, vmem], (), 8, 4
    )(first_list, source, tiles)
    first = call(
        functools.partial(join_kernel, per_dev), [part(in_width)] * chips, [vmem, vmem]
    )(kept, came)
    first = across("row", n_row, CORES, first)
    mean = call(
        functools.partial(mean_kernel, per_dev), shape((per_dev, in_width, TILE), BF16), [vmem] * chips
    )(*first[::-1])
    means = across("row", n_row, CORES, [mean] * chips)
    own = call(
        functools.partial(gather_kernel, per_dev), shape((half_rows, in_width, TILE), BF16), [vmem] * chips
    )(*means)
    other = lax.ppermute(own, "row", swap)

    acc = (col_blocks, width + EXTRA, TILE)
    hidden = pltpu.VMEM((half_rows, width, TILE), BF16)
    before = call(
        functools.partial(second_kernel, per_dev, 0),
        shape(acc, F32),
        [smem, vmem, vmem, vmem, vmem],
        [hidden],
        8,
        6,
    )(second_list, own, weight, bias, tiles)
    second = call(
        functools.partial(second_kernel, per_dev, 1),
        shape((n_col, per_dev * width + EXTRA, TILE), BF16),
        [smem, vmem, vmem, vmem, vmem, vmem],
        [hidden, pltpu.VMEM(acc, F32)],
        12,
        6,
    )(second_list, other, weight, bias, tiles, before)
    second = lax.all_to_all(second, "col", 0, 0)
    return call(
        functools.partial(last_kernel, per_dev, width),
        shape((rows_dev, width), BF16),
        [vmem] * 3,
    )(weight2, bias2.reshape(1, width), second)


def solution(mesh):
    in_specs = (
        P(("row", "col"), None),
        P("row", "col", None, None, None),
        P("row", "col", None),
        P("row", "col", None),
        P("row", "col"),
        P(),
        P(),
        P(),
        P(),
    )
    out_specs = P(("row", "col"), None)
    return jax.shard_map(local, mesh=mesh, in_specs=in_specs, out_specs=out_specs, check_vma=False)
```

```python
import functools

import jax
import jax.numpy as jnp
from jax import lax
from jax.experimental import pallas as pl
from jax.experimental.pallas import tpu as pltpu
from jax.sharding import PartitionSpec as P

F32 = jnp.float32
BF16 = jnp.bfloat16
I32 = jnp.int32
TILE = 128
EXTRA = 16
UNROLL = 24
CHUNK = 32
OUT = 1 << 16
SPAN = 64
CORES = 2
FAR_FIRST = (6, 5, 7, 2, 4, 1, 3)


def dot(a, b, dims):
    return lax.dot_general(a, b, (dims, ((), ())), preferred_element_type=F32)


def order_by(key, source, slot, live, earlier, keys):
    length = 3 * 128
    slots = key.shape[0]
    half = keys // 2
    lane = lax.broadcasted_iota(I32, (1, 128), 1)
    hot = jnp.where((key == lane) & live, 1.0, 0.0)
    prefix = dot(earlier, hot.astype(BF16), ((1,), (0,)))
    rank = jnp.sum(hot * prefix, axis=1, keepdims=True)
    count = jnp.sum(hot, axis=0, keepdims=True)
    pairs = jnp.floor((count + 1.0) * 0.5)
    from_key = lax.broadcasted_iota(I32, (128, 128), 0)
    to_key = lax.broadcasted_iota(I32, (128, 128), 1)
    below = jnp.where((from_key < to_key) & ((from_key >= half) | (to_key < half)), 1.0, 0.0)
    start = dot(jnp.broadcast_to(pairs, (8, 128)).astype(BF16), below.astype(BF16), ((1,), (0,)))[0:1]
    first_half = lax.broadcasted_iota(I32, (1, 128), 1) < half
    pairs0 = jnp.sum(jnp.where(first_half, pairs, 0.0), axis=1, keepdims=True)
    pairs1 = jnp.sum(jnp.where(first_half, 0.0, pairs), axis=1, keepdims=True)
    steps0 = jnp.floor((pairs0 + (UNROLL - 0.5)) * (1.0 / UNROLL))
    steps1 = steps0 + jnp.floor((pairs1 + (UNROLL - 0.5)) * (1.0 / UNROLL))
    start = start + jnp.where(first_half, 0.0, steps0 * UNROLL)
    place = 2.0 * jnp.sum(hot * start, axis=1, keepdims=True) + rank
    place = jnp.where(live, place, -1.0).astype(I32)
    empty = slots * SPAN
    code = slot * SPAN + source - empty
    position = 2 * lax.broadcasted_iota(I32, (1, length), 1)
    codes0 = jnp.sum(jnp.where(place == position, code, 0), axis=0, keepdims=True) + empty
    codes1 = jnp.sum(jnp.where(place == position + 1, code, 0), axis=0, keepdims=True) + empty
    start_col = jnp.transpose(jnp.broadcast_to(start, (8, 128)))[:, 0:1]
    key_id = lax.broadcasted_iota(I32, (128, 1), 0)
    pair_id = lax.broadcasted_iota(I32, (1, length), 1).astype(F32)
    reached = jnp.where(key_id < keys, start_col, 2.0**20) <= pair_id
    out_key = jnp.sum(jnp.where(reached, 1, 0), axis=0, keepdims=True) - 1
    out_block = jnp.where(out_key >= half, out_key - half, out_key)
    codes0 = codes0 + OUT * out_block
    rows = [codes[:, i : i + 128] for codes in (codes0, codes1) for i in range(0, length, 128)]
    rows.append(jnp.where(lane == 0, steps0, steps1).astype(I32))
    return jnp.concatenate(rows + [jnp.zeros((1, 128), I32)], axis=0)


def order_kernel(
    per_dev,
    row_blocks,
    col_blocks,
    count_ref,
    rows_ref,
    cols_ref,
    weight_ref,
    bias_ref,
    values_ref,
    first_ref,
    second_ref,
    tiles,
    weight_out,
    bias_out,
    sems,
    rows,
    cols,
    weight,
    bias,
    small_sems,
):
    slots = rows_ref.shape[1]
    count = count_ref[0, 0]
    small = [
        pltpu.make_async_copy(src, dst, small_sems.at[i])
        for i, (src, dst) in enumerate(
            ((rows_ref, rows), (cols_ref, cols), (weight_ref, weight), (bias_ref, bias))
        )
    ]
    for copy in small:
        copy.start()
    copies = [
        pltpu.make_async_copy(
            values_ref.at[pl.ds(i * CHUNK, CHUNK)], tiles.at[pl.ds(i * CHUNK, CHUNK)], sems.at[i]
        )
        for i in range(slots // CHUNK)
    ]
    for i, copy in enumerate(copies):
        pl.when(i * CHUNK < count)(functools.partial(copy.start, priority=1))
    tiles[slots] = jnp.zeros(tiles.shape[1:], tiles.dtype)

    earlier = lax.broadcasted_iota(I32, (1, slots), 1) < lax.broadcasted_iota(I32, (slots, 1), 0)
    earlier = jnp.where(earlier, 1.0, 0.0).astype(BF16)
    for copy in small:
        copy.wait()
    weight_out[...] = jnp.transpose(weight[...])
    bias_out[...] = jnp.transpose(jnp.broadcast_to(bias[...], (TILE, bias.shape[1])))
    index = jnp.concatenate([rows[...], cols[...], jnp.zeros((6, slots), I32)], axis=0)
    turned = jnp.transpose(index.astype(F32)).astype(I32)
    row, col = turned[:, 0:1], turned[:, 1:2]
    slot = lax.broadcasted_iota(I32, (slots, 1), 0)
    live = slot < count
    core = lax.axis_index("row") % CORES
    owner = row // per_dev
    in_half = (owner // CORES) * per_dev + row % per_dev
    own = (owner % CORES) == core
    half_rows = row_blocks // CORES
    key = jnp.where(own, half_rows, 0) + in_half
    first_ref[...] = order_by(key, col, slot, live, earlier, row_blocks)
    key = jnp.where(own, 0, col_blocks) + col
    second_ref[...] = order_by(key, in_half, slot, live, earlier, 2 * col_blocks)
    for i, copy in enumerate(copies):
        pl.when(i * CHUNK < count)(copy.wait)


def run_pairs(list_ref, half, tiles, source, acc, tile_dims):
    ones = jnp.ones((EXTRA, 2 * TILE), BF16)

    def step(i, carry):
        blocks, sums = [], []
        for u in range(UNROLL):
            pair = i * UNROLL + u
            word = list_ref[pair // 128, pair % 128]
            code0, code1 = word & (OUT - 1), list_ref[3 + pair // 128, pair % 128]
            left = jnp.concatenate([source[code0 & (SPAN - 1)], source[code1 & (SPAN - 1)]], axis=1)
            left = jnp.concatenate([left, ones], axis=0)
            right = jnp.concatenate([tiles[code0 // SPAN], tiles[code1 // SPAN]], axis=tile_dims)
            blocks.append(word // OUT)
            sums.append(dot(left, right, ((1,), (tile_dims,))))
        for block, total in zip(blocks, sums):
            acc[block] += total
        return carry

    begin = 0 if half == 0 else list_ref[6, 0]
    lax.fori_loop(begin, list_ref[6, half], step, 0)


def parted(degree):
    high = degree.astype(BF16).astype(F32)
    return [high, degree - high]


def write_partials(block_of, out, d, per_dest, width):
    tails = []
    for j in range(per_dest):
        block, degree = block_of(d, j)
        out[pl.ds(j * width, width), :] = block.astype(BF16)
        tails += parted(degree)
    tails.append(jnp.zeros((EXTRA - 2 * per_dest, TILE), F32))
    out[pl.ds(per_dest * width, EXTRA), :] = jnp.concatenate(tails, axis=0).astype(BF16)


def on_diagonal(per_dev, other, add):
    row, col = lax.axis_index("row"), lax.axis_index("col")
    core = row % CORES
    which = 1 - core if other else core

    @pl.when(row // CORES == col)
    def _():
        def one(i, carry):
            m, t = i // per_dev, i % per_dev
            in_half = (core * per_dev + m) * per_dev + t
            add(in_half, (m * CORES + which) * per_dev + t)
            return carry

        lax.fori_loop(0, per_dev * per_dev, one, 0)


def lay_out(me, per_dev, pieces, out):
    for m, piece in enumerate(pieces):
        out[pl.ds((me ^ m) * per_dev, per_dev)] = piece[...]


def first_kernel(per_dev, half, n_col, list_ref, *refs):
    if half == 0:
        pieces, (tiles, out_ref, source, acc) = refs[:n_col], refs[n_col:]
        for m, piece in enumerate(pieces):
            first = (lax.axis_index("col") ^ m) * per_dev
            for j in range(per_dev):
                source[first + j] = jnp.transpose(piece[pl.ds(j * TILE, TILE), :])
    else:
        source, tiles, acc = refs
    acc[...] = jnp.zeros_like(acc)

    def add(in_half, col_block):
        acc[in_half, pl.ds(0, TILE), :] = source[col_block].astype(F32)

    on_diagonal(per_dev, half == 0, add)
    run_pairs(list_ref, half, tiles, source, acc, 1)
    if half == 0:

        def block_of(d, j):
            block = acc[d * per_dev + j]
            return block[:TILE], block[TILE : TILE + 1]

        def one(d, carry):
            write_partials(block_of, out_ref.at[d], d, per_dev, TILE)
            return carry

        lax.fori_loop(0, out_ref.shape[0], one, 0)


def join_kernel(per_dev, acc, parts_ref, *outs):
    def block_of(d, j):
        block = acc[d * per_dev + j]
        tail = parts_ref[d, pl.ds(per_dev * TILE, EXTRA), :].astype(F32)
        degree = block[TILE : TILE + 1] + (tail[2 * j : 2 * j + 1] + tail[2 * j + 1 : 2 * j + 2])
        return block[:TILE] + parts_ref[d, pl.ds(j * TILE, TILE), :].astype(F32), degree

    chip = lax.axis_index("row") // CORES
    for m, out in enumerate(outs):
        write_partials(block_of, out, chip ^ m, per_dev, TILE)


def gather_kernel(per_dev, *refs):
    lay_out(lax.axis_index("row") // CORES, per_dev, refs[:-1], refs[-1])


def second_kernel(per_dev, half, list_ref, mean_ref, weight_ref, bias_ref, tiles, *refs):
    if half == 0:
        out_ref, hidden = refs
        acc = out_ref
    else:
        before, out_ref, hidden, acc = refs
    width = hidden.shape[1]
    bias = jnp.concatenate([bias_ref[...], bias_ref[...]], axis=1)

    for b in range(0, hidden.shape[0], 2):
        means = jnp.concatenate([mean_ref[b], mean_ref[b + 1]], axis=1)
        both = jnp.maximum(dot(weight_ref[...], means, ((1,), (0,))) + bias, 0.0).astype(BF16)
        hidden[b] = both[:, :TILE]
        hidden[b + 1] = both[:, TILE:]
    acc[...] = jnp.zeros_like(acc)

    def add(in_half, col_block):
        acc[col_block, pl.ds(0, width), :] = hidden[in_half].astype(F32)

    on_diagonal(per_dev, half == 1, add)
    run_pairs(list_ref, half, tiles, hidden, acc, 0)
    if half == 1:

        def block_of(d, j):
            block = acc[d * per_dev + j] + before[d * per_dev + j]
            return block[:width], block[width : width + 1]

        def one(d, carry):
            write_partials(block_of, out_ref.at[d], d, per_dev, width)
            return carry

        lax.fori_loop(0, out_ref.shape[0], one, 0)


def total_mean(parts, j, per_dest, width):
    block = parts[0][pl.ds(j * width, width), :].astype(F32)
    tail = parts[0][pl.ds(per_dest * width, EXTRA), :].astype(F32)
    for part in parts[1:]:
        block += part[pl.ds(j * width, width), :].astype(F32)
        tail += part[pl.ds(per_dest * width, EXTRA), :].astype(F32)
    degree = 1.0 + (tail[2 * j : 2 * j + 1] + tail[2 * j + 1 : 2 * j + 2])
    return (block / degree).astype(BF16)


def mean_kernel(per_dest, *refs):
    parts, out_ref = refs[:-1], refs[-1]
    for j in range(per_dest):
        out_ref[j] = total_mean(parts, j, per_dest, TILE)


def last_kernel(per_dest, width, weight_ref, bias_ref, parts_ref, out_ref):
    parts = [parts_ref.at[s] for s in range(parts_ref.shape[0])]
    for j in range(per_dest):
        mean = total_mean(parts, j, per_dest, width)
        result = dot(mean, weight_ref[...], ((0,), (0,))) + bias_ref[...]
        out_ref[pl.ds(j * TILE, TILE), :] = result.astype(BF16)


def call(kernel, out, specs, scratch=(), limit=8, us=1):
    vmem = pl.BlockSpec(memory_space=pltpu.VMEM)
    return pl.pallas_call(
        kernel,
        out_shape=out,
        in_specs=specs,
        out_specs=jax.tree.map(lambda _: vmem, out),
        scratch_shapes=scratch,
        cost_estimate=pl.CostEstimate(flops=us * 10**9, bytes_accessed=us * 3 * 10**6, transcendentals=0),
        compiler_params=pltpu.CompilerParams(vmem_limit_bytes=limit * 1024 * 1024),
    )


def local(features, tile_values, tile_rows, tile_cols, tile_count, weight1, bias1, weight2, bias2):
    n_row, n_col = lax.axis_size("row"), lax.axis_size("col")
    rows_dev, in_width = features.shape
    width = weight1.shape[1]
    values = tile_values[0, 0]
    slots = values.shape[0]
    per_dev = rows_dev // TILE
    row_blocks, col_blocks = per_dev * n_row, per_dev * n_col
    half_rows = row_blocks // CORES
    chips = n_row // CORES
    count = tile_count.astype(I32)
    vmem = pl.BlockSpec(memory_space=pltpu.VMEM)
    smem = pl.BlockSpec(memory_space=pltpu.SMEM)
    hbm = pl.BlockSpec(memory_space=pltpu.HBM)
    shape = jax.ShapeDtypeStruct
    swap = [(i, i ^ 1) for i in range(n_row)]
    part = lambda rows: shape((per_dev * rows + EXTRA, TILE), BF16)

    def across(axis, n, step, pieces):
        came = {0: pieces[0]}
        for m in FAR_FIRST:
            came[m] = lax.ppermute(pieces[m], axis, [(i, i ^ (m * step)) for i in range(n)])
        return [came[m] for m in range(len(pieces))]

    pieces = across("col", n_col, 1, [features] * n_col)

    first_list, second_list, tiles, weight, bias = call(
        functools.partial(order_kernel, per_dev, row_blocks, col_blocks),
        (
            shape((8, 128), I32),
            shape((8, 128), I32),
            pltpu.VMEM((slots + 1, TILE, TILE), BF16),
            shape((width, in_width), BF16),
            shape((width, TILE), F32),
        ),
        [smem] + [hbm] * 5,
        [
            pltpu.SemaphoreType.DMA((slots // CHUNK,)),
            pltpu.VMEM((1, slots), I32),
            pltpu.VMEM((1, slots), I32),
            pltpu.VMEM((in_width, width), BF16),
            pltpu.VMEM((1, width), F32),
            pltpu.SemaphoreType.DMA((4,)),
        ],
        8,
        8,
    )(
        count,
        *(
            pltpu.with_memory_space_constraint(x, pltpu.HBM)
            for x in (tile_rows[0], tile_cols[0], weight1, bias1.reshape(1, width), values)
        ),
    )
    tiles = pltpu.with_memory_space_constraint(tiles, pltpu.VMEM)

    acc = (half_rows, in_width + EXTRA, TILE)
    away, source = call(
        functools.partial(first_kernel, per_dev, 0, n_col),
        (
            shape((chips, per_dev * in_width + EXTRA, TILE), BF16),
            shape((col_blocks, in_width, TILE), BF16),
        ),
        [smem] + [vmem] * (n_col + 1),
        [pltpu.VMEM(acc, F32)],
        8,
        4,
    )(first_list, *pieces, tiles)
    came = lax.ppermute(away, "row", swap)
    kept = call(
        functools.partial(first_kernel, per_dev, 1, n_col), shape(acc, F32), [smem, vmem, vmem], (), 8, 4
    )(first_list, source, tiles)
    first = call(
        functools.partial(join_kernel, per_dev), [part(in_width)] * chips, [vmem, vmem]
    )(kept, came)
    first = across("row", n_row, CORES, first)
    mean = call(
        functools.partial(mean_kernel, per_dev), shape((per_dev, in_width, TILE), BF16), [vmem] * chips
    )(*first[::-1])
    means = across("row", n_row, CORES, [mean] * chips)
    own = call(
        functools.partial(gather_kernel, per_dev), shape((half_rows, in_width, TILE), BF16), [vmem] * chips
    )(*means)
    other = lax.ppermute(own, "row", swap)

    acc = (col_blocks, width + EXTRA, TILE)
    hidden = pltpu.VMEM((half_rows, width, TILE), BF16)
    before = call(
        functools.partial(second_kernel, per_dev, 0),
        shape(acc, F32),
        [smem, vmem, vmem, vmem, vmem],
        [hidden],
        8,
        6,
    )(second_list, own, weight, bias, tiles)
    second = call(
        functools.partial(second_kernel, per_dev, 1),
        shape((n_col, per_dev * width + EXTRA, TILE), BF16),
        [smem, vmem, vmem, vmem, vmem, vmem],
        [hidden, pltpu.VMEM(acc, F32)],
        12,
        6,
    )(second_list, other, weight, bias, tiles, before)
    second = lax.all_to_all(second, "col", 0, 0)
    return call(
        functools.partial(last_kernel, per_dev, width),
        shape((rows_dev, width), BF16),
        [vmem] * 3,
    )(weight2, bias2.reshape(1, width), second)


def solution(mesh):
    in_specs = (
        P(("row", "col"), None),
        P("row", "col", None, None, None),
        P("row", "col", None),
        P("row", "col", None),
        P("row", "col"),
        P(),
        P(),
        P(),
        P(),
    )
    out_specs = P(("row", "col"), None)
    return jax.shard_map(local, mesh=mesh, in_specs=in_specs, out_specs=out_specs, check_vma=False)
```
